32 devices in a mesh: dp: 8 (over z, core), fsdp: 4 (over y, x).
Axes of the slice: x: 2, y: 2, z: 4, core: 2. Of those that a mesh axis runs over, the one named last changes fastest.
Arguments:
- big_crops: bfloat16 [128, 28, 28, 192], P(('dp', 'fsdp')), may hold values from -15 to 15
- small_crops: bfloat16 [384, 12, 12, 192], P(('dp', 'fsdp')), may hold values from -15 to 15
- big_cot: bfloat16 [128, 14, 14, 512], P(('dp', 'fsdp')), may hold values from -15 to 15
- small_cot: bfloat16 [384, 6, 6, 512], P(('dp', 'fsdp')), may hold values from -15 to 15
- enter_one: bfloat16 [98304], P(('dp', 'fsdp')), may hold values from -0.4375 to 0.4375
- engain_one: float32 [512], replicated, may hold values from 0.25 to 1.75
- enbias_one: float32 [512], replicated, may hold values from -3 to 3
- group_one: bfloat16 [294912], P(('dp', 'fsdp')), may hold values from -0.25 to 0.25
- grgain_one: float32 [512], replicated, may hold values from 0.25 to 1.75
- grbias_one: float32 [512], replicated, may hold values from -3 to 3
- sqdown_one: bfloat16 [24576], P(('dp', 'fsdp')), may hold values from -0.75 to 0.75
- sqdbias_one: float32 [48], replicated, may hold values from -3 to 3
- squp_one: bfloat16 [24576], P(('dp', 'fsdp')), may hold values from -1.75 to 1.75
- squbias_one: float32 [512], replicated, may hold values from -3 to 3
- leave_one: bfloat16 [262144], P(('dp', 'fsdp')), may hold values from -0.25 to 0.25
- lvgain_one: float32 [512], replicated, may hold values from 0.25 to 1.75
- lvbias_one: float32 [512], replicated, may hold values from -3 to 3
- shortcut_one: bfloat16 [98304], P(('dp', 'fsdp')), may hold values from -0.4375 to 0.4375
- scgain_one: float32 [512], replicated, may hold values from 0.25 to 1.75
- scbias_one: float32 [512], replicated, may hold values from -3 to 3
- enter_two: bfloat16 [262144], P(('dp', 'fsdp')), may hold values from -0.25 to 0.25
- engain_two: float32 [512], replicated, may hold values from 0.25 to 1.75
- enbias_two: float32 [512], replicated, may hold values from -3 to 3
- group_two: bfloat16 [294912], P(('dp', 'fsdp')), may hold values from -0.25 to 0.25
- grgain_two: float32 [512], replicated, may hold values from 0.25 to 1.75
- grbias_two: float32 [512], replicated, may hold values from -3 to 3
- sqdown_two: bfloat16 [65536], P(('dp', 'fsdp')), may hold values from -0.75 to 0.75
- sqdbias_two: float32 [128], replicated, may hold values from -3 to 3
- squp_two: bfloat16 [65536], P(('dp', 'fsdp')), may hold values from -1 to 1
- squbias_two: float32 [512], replicated, may hold values from -3 to 3
- leave_two: bfloat16 [262144], P(('dp', 'fsdp')), may hold values from -0.25 to 0.25
- lvgain_two: float32 [512], replicated, may hold values from 0.25 to 1.75
- lvbias_two: float32 [512], replicated, may hold values from -3 to 3
Outputs:
- big_out: bfloat16 [128, 14, 14, 512], P(('dp', 'fsdp'))
- small_out: bfloat16 [384, 6, 6, 512], P(('dp', 'fsdp'))
- dbig_crops: bfloat16 [128, 28, 28, 192], P(('dp', 'fsdp'))
- dsmall_crops: bfloat16 [384, 12, 12, 192], P(('dp', 'fsdp'))
- denter_one: float32 [98304], P(('dp', 'fsdp'))
- dengain_one: float32 [512], replicated
- denbias_one: float32 [512], replicated
- dgroup_one: float32 [294912], P(('dp', 'fsdp'))
- dgrgain_one: float32 [512], replicated
- dgrbias_one: float32 [512], replicated
- dsqdown_one: float32 [24576], P(('dp', 'fsdp'))
- dsqdbias_one: float32 [48], replicated
- dsqup_one: float32 [24576], P(('dp', 'fsdp'))
- dsqubias_one: float32 [512], replicated
- dleave_one: float32 [262144], P(('dp', 'fsdp'))
- dlvgain_one: float32 [512], replicated
- dlvbias_one: float32 [512], replicated
- dshortcut_one: float32 [98304], P(('dp', 'fsdp'))
- dscgain_one: float32 [512], replicated
- dscbias_one: float32 [512], replicated
- denter_two: float32 [262144], P(('dp', 'fsdp'))
- dengain_two: float32 [512], replicated
- denbias_two: float32 [512], replicated
- dgroup_two: float32 [294912], P(('dp', 'fsdp'))
- dgrgain_two: float32 [512], replicated
- dgrbias_two: float32 [512], replicated
- dsqdown_two: float32 [65536], P(('dp', 'fsdp'))
- dsqdbias_two: float32 [128], replicated
- dsqup_two: float32 [65536], P(('dp', 'fsdp'))
- dsqubias_two: float32 [512], replicated
- dleave_two: float32 [262144], P(('dp', 'fsdp'))
- dlvgain_two: float32 [512], replicated
- dlvbias_two: float32 [512], replicated
The draws below stay inside these ranges and needn't reach their ends.
All inputs are finite; a program needn't handle non-finite values.
Results may differ from the reference program's by a relative error of at most 0.015.
Values may be sent and summed in bfloat16 or wider, within the bound.
No kernel may reach another device: no remote copies, remote signals or barrier semaphores. Data moves between devices by JAX's collectives and lax.ppermute only.
A program may use at most 320 MiB of HBM per device.

```python
import jax
import jax.numpy as jnp
from jax import lax

C_IN = 192
GWIDTH = 64
GROUPS = 8
WIDTH = 512
SE_ONE = 48
SE_TWO = 128
BIG_OUT = 14
SMALL_OUT = 6
BIG_CROPS = 2
SMALL_CROPS = 6
IMAGES = 64


def shaped_field(key, base_vals, num_rows, per_image, channels, log_spread):
    image_idx = jnp.arange(num_rows) // per_image
    rising = 0.5 + image_idx.astype(jnp.float32) / max(IMAGES - 1, 1)
    chan_scale = jnp.exp(jax.random.uniform(jax.random.fold_in(key, 7), (channels,), jnp.float32, -log_spread, log_spread))
    return base_vals * rising[:, None, None, None] * chan_scale


def draw_big_crops(key, part):
    key = jax.random.fold_in(key, 1)
    dims_all = (IMAGES * BIG_CROPS, 2 * BIG_OUT, 2 * BIG_OUT, C_IN)
    base_vals = jnp.clip(jax.random.normal(key, dims_all, jnp.float32), -4.0, 4.0)
    log_spread = 0.9
    return shaped_field(key, base_vals, IMAGES * BIG_CROPS, BIG_CROPS, C_IN, log_spread).astype(jnp.bfloat16)


def draw_small_crops(key, part):
    key = jax.random.fold_in(key, 2)
    dims_all = (IMAGES * SMALL_CROPS, 2 * SMALL_OUT, 2 * SMALL_OUT, C_IN)
    base_vals = jnp.clip(jax.random.normal(key, dims_all, jnp.float32), -4.0, 4.0)
    log_spread = 0.9
    return shaped_field(key, base_vals, IMAGES * SMALL_CROPS, SMALL_CROPS, C_IN, log_spread).astype(jnp.bfloat16)


def draw_big_cot(key, part):
    key = jax.random.fold_in(key, 3)
    dims_all = (IMAGES * BIG_CROPS, BIG_OUT, BIG_OUT, GROUPS * GWIDTH)
    base_vals = jnp.clip(jax.random.normal(key, dims_all, jnp.float32), -4.0, 4.0)
    log_spread = 0.9
    return shaped_field(key, base_vals, IMAGES * BIG_CROPS, BIG_CROPS, GROUPS * GWIDTH, log_spread).astype(jnp.bfloat16)


def draw_small_cot(key, part):
    key = jax.random.fold_in(key, 4)
    dims_all = (IMAGES * SMALL_CROPS, SMALL_OUT, SMALL_OUT, GROUPS * GWIDTH)
    base_vals = jnp.clip(jax.random.normal(key, dims_all, jnp.float32), -4.0, 4.0)
    log_spread = 0.9
    return shaped_field(key, base_vals, IMAGES * SMALL_CROPS, SMALL_CROPS, GROUPS * GWIDTH, log_spread).astype(jnp.bfloat16)


def block_levels(key, shape, cuts, low, high):
    level = 1.0
    for position, parts in cuts:
        heights = jax.random.uniform(jax.random.fold_in(jax.random.fold_in(key, 6), position), (parts,), jnp.float32, low / len(cuts), high / len(cuts))
        level = level * jnp.repeat(jnp.exp(heights), shape[position] // parts).reshape((-1,) + (1,) * (len(shape) - 1 - position))
    return level


def gaussian(rng, shape, width, most, split=(), kind=jnp.bfloat16):
    loudness = block_levels(rng, shape, split, -0.22, 0.18) if split else 1.0
    values = jax.random.normal(rng, shape, jnp.float32) * width * loudness
    return jnp.minimum(jnp.maximum(values, -most), most).astype(kind)


def setup_inputs(seed: int = 0) -> dict:
    keys = jax.random.split(jax.random.key(seed), 34)
    return {
        "big_crops": draw_big_crops(jax.random.fold_in(keys[33], 71), 0),
        "small_crops": draw_small_crops(jax.random.fold_in(keys[33], 71), 0),
        "big_cot": draw_big_cot(jax.random.fold_in(keys[33], 71), 0),
        "small_cot": draw_small_cot(jax.random.fold_in(keys[33], 71), 0),
        "enter_one": gaussian(keys[4], (C_IN * WIDTH,), C_IN ** -0.5, 0.4375, ((0, 32),)),
        "engain_one": jnp.clip(1.0 + 0.15 * jax.random.normal(keys[5], (WIDTH,), jnp.float32), 0.25, 1.75),
        "enbias_one": gaussian(keys[6], (WIDTH,), 0.3, 3.0, (), jnp.float32),
        "group_one": gaussian(keys[7], (9 * WIDTH * GWIDTH,), (9 * GWIDTH) ** -0.5, 0.25, ((0, 32),)),
        "grgain_one": jnp.clip(1.0 + 0.15 * jax.random.normal(keys[8], (WIDTH,), jnp.float32), 0.25, 1.75),
        "grbias_one": gaussian(keys[9], (WIDTH,), 0.3, 3.0, (), jnp.float32),
        "sqdown_one": gaussian(keys[10], (WIDTH * SE_ONE,), (WIDTH // 8) ** -0.5, 0.75, ((0, 32),)),
        "sqdbias_one": gaussian(keys[11], (SE_ONE,), 0.5, 3.0, (), jnp.float32),
        "squp_one": gaussian(keys[12], (SE_ONE * WIDTH,), (SE_ONE // 4) ** -0.5, 1.75, ((0, 32),)),
        "squbias_one": gaussian(keys[13], (WIDTH,), 0.5, 3.0, (), jnp.float32),
        "leave_one": gaussian(keys[14], (WIDTH * WIDTH,), WIDTH ** -0.5, 0.25, ((0, 32),)),
        "lvgain_one": jnp.clip(1.0 + 0.15 * jax.random.normal(keys[15], (WIDTH,), jnp.float32), 0.25, 1.75),
        "lvbias_one": gaussian(keys[16], (WIDTH,), 0.3, 3.0, (), jnp.float32),
        "shortcut_one": gaussian(keys[17], (C_IN * WIDTH,), C_IN ** -0.5, 0.4375, ((0, 32),)),
        "scgain_one": jnp.clip(1.0 + 0.15 * jax.random.normal(keys[18], (WIDTH,), jnp.float32), 0.25, 1.75),
        "scbias_one": gaussian(keys[19], (WIDTH,), 0.3, 3.0, (), jnp.float32),
        "enter_two": gaussian(keys[20], (WIDTH * WIDTH,), WIDTH ** -0.5, 0.25, ((0, 32),)),
        "engain_two": jnp.clip(1.0 + 0.15 * jax.random.normal(keys[21], (WIDTH,), jnp.float32), 0.25, 1.75),
        "enbias_two": gaussian(keys[22], (WIDTH,), 0.3, 3.0, (), jnp.float32),
        "group_two": gaussian(keys[23], (9 * WIDTH * GWIDTH,), (9 * GWIDTH) ** -0.5, 0.25, ((0, 32),)),
        "grgain_two": jnp.clip(1.0 + 0.15 * jax.random.normal(keys[24], (WIDTH,), jnp.float32), 0.25, 1.75),
        "grbias_two": gaussian(keys[25], (WIDTH,), 0.3, 3.0, (), jnp.float32),
        "sqdown_two": gaussian(keys[26], (WIDTH * SE_TWO,), (WIDTH // 8) ** -0.5, 0.75, ((0, 32),)),
        "sqdbias_two": gaussian(keys[27], (SE_TWO,), 0.5, 3.0, (), jnp.float32),
        "squp_two": gaussian(keys[28], (SE_TWO * WIDTH,), (SE_TWO // 4) ** -0.5, 1.0, ((0, 32),)),
        "squbias_two": gaussian(keys[29], (WIDTH,), 0.5, 3.0, (), jnp.float32),
        "leave_two": gaussian(keys[30], (WIDTH * WIDTH,), WIDTH ** -0.5, 0.25, ((0, 32),)),
        "lvgain_two": jnp.clip(1.0 + 0.15 * jax.random.normal(keys[31], (WIDTH,), jnp.float32), 0.25, 1.75),
        "lvbias_two": gaussian(keys[32], (WIDTH,), 0.3, 3.0, (), jnp.float32),
    }


@jax.custom_vjp
def low(v):
    return lax.optimization_barrier(v.astype(jnp.bfloat16)).astype(jnp.float32)

@jax.custom_vjp
def low_back(v):
    return v

def low_keep(v):
    return (low(v), None)

def low_pass(kept, grad):
    return (grad,)

def back_keep(v):
    return (v, None)

def back_low(kept, grad):
    return (low(grad),)
low.defvjp(low_keep, low_pass)
low_back.defvjp(back_keep, back_low)
epsilon = 1e-05
highest = lax.Precision.HIGHEST

def flat_rows(values):
    return values.reshape(-1, values.shape[-1])

def matmul_rows(features, weight):
    result = jnp.dot(flat_rows(features), weight, precision=highest, preferred_element_type=jnp.float32)
    return result.reshape(features.shape[:-1] + (weight.shape[1],))

def tap_slice(padded, tap_idx, stride, out_rows, out_cols):
    row_off, col_off = divmod(tap_idx, 3)
    return padded[:, row_off:row_off + stride * (out_rows - 1) + 1:stride, col_off:col_off + stride * (out_cols - 1) + 1:stride, :]

def group_conv(features, kernel, stride):
    num_crops, height, width_px, channels = features.shape
    groups = kernel.shape[1]
    out_h = height // stride
    out_w = width_px // stride
    padded = jnp.pad(features, ((0, 0), (1, 1), (1, 1), (0, 0)))
    summed = jnp.zeros((num_crops, out_h, out_w, groups, channels // groups), jnp.float32)
    for tap_idx in range(9):
        window = tap_slice(padded, tap_idx, stride, out_h, out_w).reshape(num_crops, out_h, out_w, groups, channels // groups)
        summed = summed + jnp.einsum('nhwgc,gcd->nhwgd', window, kernel[tap_idx], precision=highest, preferred_element_type=jnp.float32)
    return summed.reshape(num_crops, out_h, out_w, channels)

def batch_norm(pieces, norm_gain, norm_shift):
    count_all = sum((flat_rows(member).shape[0] for member in pieces))
    centre = sum((lax.optimization_barrier(jnp.sum(flat_rows(member), axis=0)) for member in pieces)) / count_all
    variance = sum((lax.optimization_barrier(jnp.sum(jnp.square(flat_rows(member) - centre), axis=0)) for member in pieces)) / count_all
    inv_std = lax.rsqrt(variance + epsilon)
    return [(member - centre) * inv_std * norm_gain + norm_shift for member in pieces]

def squeeze_pair(feature_list, down_w, down_bias, up_w, up_bias):
    result = []
    for features in feature_list:
        pooled = lax.optimization_barrier(jnp.mean(features, axis=(1, 2)))
        hidden = jax.nn.silu(jnp.dot(pooled, down_w, precision=highest) + down_bias)
        gating = jax.nn.sigmoid(jnp.dot(hidden, up_w, precision=highest) + up_bias)
        result.append(features * gating[:, None, None, :])
    return result

def first_block(crops, weights):
    enter_w, en_gain, en_bias, group_w, gr_gain, gr_bias, down_w, down_bias, up_w, up_bias, leave_w, lv_gain, lv_bias, short_w, sc_gain, sc_bias = weights
    enter_mat = enter_w.reshape(C_IN, WIDTH)
    kernel = group_w.reshape(9, GROUPS, GWIDTH, GWIDTH)
    down_mat = down_w.reshape(WIDTH, SE_ONE)
    up_mat = up_w.reshape(SE_ONE, WIDTH)
    leave_mat = leave_w.reshape(WIDTH, WIDTH)
    short_mat = short_w.reshape(C_IN, WIDTH)
    entered = [low_back(matmul_rows(member, enter_mat)) for member in crops]
    acts_enter = [low(jax.nn.silu(member)) for member in batch_norm(entered, en_gain, en_bias)]
    grouped = [low_back(group_conv(member, kernel, 2)) for member in acts_enter]
    acts_group = [jax.nn.silu(member) for member in batch_norm(grouped, gr_gain, gr_bias)]
    scaled = [low(member) for member in squeeze_pair(acts_group, down_mat, down_bias, up_mat, up_bias)]
    leave_out = batch_norm([low_back(matmul_rows(member, leave_mat)) for member in scaled], lv_gain, lv_bias)
    skip_out = batch_norm([low_back(matmul_rows(member[:, ::2, ::2, :], short_mat)) for member in crops], sc_gain, sc_bias)
    return [jax.nn.silu(one_side + other_side) for one_side, other_side in zip(leave_out, skip_out)]

def second_block(inputs, weights):
    enter_w, en_gain, en_bias, group_w, gr_gain, gr_bias, down_w, down_bias, up_w, up_bias, leave_w, lv_gain, lv_bias = weights
    enter_mat = enter_w.reshape(WIDTH, WIDTH)
    kernel = group_w.reshape(9, GROUPS, GWIDTH, GWIDTH)
    down_mat = down_w.reshape(WIDTH, SE_TWO)
    up_mat = up_w.reshape(SE_TWO, WIDTH)
    leave_mat = leave_w.reshape(WIDTH, WIDTH)
    lowered = [low(member) for member in inputs]
    entered = [low_back(matmul_rows(member, enter_mat)) for member in lowered]
    acts_enter = [low(jax.nn.silu(member)) for member in batch_norm(entered, en_gain, en_bias)]
    grouped = [low_back(group_conv(member, kernel, 1)) for member in acts_enter]
    acts_group = [jax.nn.silu(member) for member in batch_norm(grouped, gr_gain, gr_bias)]
    scaled = [low(member) for member in squeeze_pair(acts_group, down_mat, down_bias, up_mat, up_bias)]
    leave_out = batch_norm([low_back(matmul_rows(member, leave_mat)) for member in scaled], lv_gain, lv_bias)
    return [jax.nn.silu(one_side + other_side) for one_side, other_side in zip(leave_out, inputs)]

def reference(big_crops, small_crops, big_cot, small_cot, enter_one, engain_one, enbias_one, group_one, grgain_one, grbias_one, sqdown_one, sqdbias_one, squp_one, squbias_one, leave_one, lvgain_one, lvbias_one, shortcut_one, scgain_one, scbias_one, enter_two, engain_two, enbias_two, group_two, grgain_two, grbias_two, sqdown_two, sqdbias_two, squp_two, squbias_two, leave_two, lvgain_two, lvbias_two):
    first_args = (enter_one, engain_one, enbias_one, group_one, grgain_one, grbias_one, sqdown_one, sqdbias_one, squp_one, squbias_one, leave_one, lvgain_one, lvbias_one, shortcut_one, scgain_one, scbias_one)
    second_args = (enter_two, engain_two, enbias_two, group_two, grgain_two, grbias_two, sqdown_two, sqdbias_two, squp_two, squbias_two, leave_two, lvgain_two, lvbias_two)
    first_float = tuple((member.astype(jnp.float32) for member in first_args))
    second_float = tuple((member.astype(jnp.float32) for member in second_args))

    def whole(big_in, small_in, first_weights, second_weights):
        middle = jax.checkpoint(first_block)([big_in, small_in], first_weights)
        result = jax.checkpoint(second_block)(middle, second_weights)
        return (result[0], result[1])
    primal, pullback = jax.vjp(whole, big_crops.astype(jnp.float32), small_crops.astype(jnp.float32), first_float, second_float)
    d_big, d_small, d_first, d_second = pullback((big_cot.astype(jnp.float32), small_cot.astype(jnp.float32)))
    return (primal[0].astype(jnp.bfloat16), primal[1].astype(jnp.bfloat16), d_big.astype(jnp.bfloat16), d_small.astype(jnp.bfloat16), d_first[0], d_first[1], d_first[2], d_first[3], d_first[4], d_first[5], d_first[6], d_first[7], d_first[8], d_first[9], d_first[10], d_first[11], d_first[12], d_first[13], d_first[14], d_first[15], d_second[0], d_second[1], d_second[2], d_second[3], d_second[4], d_second[5], d_second[6], d_second[7], d_second[8], d_second[9], d_second[10], d_second[11], d_second[12])
```

```python
import functools
from typing import NamedTuple

import jax
import jax.numpy as jnp
from jax import lax
from jax.experimental import pallas as pl
from jax.experimental.pallas import tpu as pltpu
from jax.sharding import PartitionSpec as P

AXES = ("dp", "fsdp")
C_IN = 192
GWIDTH = 64
GROUPS = 8
WIDTH = 512
SE_ONE = 48
SE_TWO = 128
HALF = 256
EPS = 1e-05
HIGHEST = lax.Precision.HIGHEST
F32 = jnp.float32
BF16 = jnp.bfloat16
VMEM_BYTES = 58 * 2**20
SLACK_BYTES = 6 * 2**20


class Lay(NamedTuple):
    nd: int
    nb: int
    ns: int
    sb: int
    ss: int

    @property
    def pairs(self):
        return self.ns // 2

    @property
    def crops(self):
        return self.nb + self.ns

    @property
    def units_big(self):
        return self.nb * self.sb

    @property
    def rows(self):
        return 16 * (self.nb * self.sb + self.pairs * self.ss)

    @property
    def pad_big(self):
        return self.nb * (self.sb + 1) + 1

    @property
    def pad_units(self):
        return self.pad_big + self.pairs * (self.ss + 1) + 1

    @property
    def vrows(self):
        return 16 * (self.pad_units - 2)

    @property
    def vwide(self):
        return -(-self.vrows // 128) * 128

    @property
    def urows(self):
        return self.vwide + 32

    @property
    def count(self):
        return self.nb * self.sb**2 + self.ns * self.ss**2


def chunk_of(rows, most):
    units = rows // 16
    return 16 * max(d for d in range(1, units + 1) if units % d == 0 and 16 * d <= most)


def walk(g, fn, carry, inner=None, done=None):
    def outer(kind, seg, carry):
        side = g.ss if kind else g.sb
        first = g.units_big + seg * g.ss if kind else seg * g.sb
        padded = g.pad_big + seg * (g.ss + 1) + 1 if kind else seg * (g.sb + 1) + 1
        start = inner(kind) if inner else jnp.int32(0)

        def step(k, both):
            r = pl.multiple_of((first + 2 * k) * 16, 16)
            u = pl.multiple_of((padded + 2 * k) * 16, 16)
            return fn(both[0], both[1], kind, seg, r, u)

        carry, end = lax.fori_loop(0, side // 2, step, (carry, start))
        return done(kind, seg, carry, end) if done else carry

    carry = lax.fori_loop(0, g.nb, functools.partial(outer, 0), carry)
    return lax.fori_loop(0, g.pairs, functools.partial(outer, 1), carry)


def valid(g, kind, x):
    row = lax.broadcasted_iota(jnp.int32, x.shape, 0)
    keep = (row & 7) < g.ss if kind else (row & 15) < g.sb
    return jnp.where(keep, x, 0.0)


def fold(x):
    return x[0:8] + x[8:16] + x[16:24] + x[24:32]


def total(x):
    return jnp.sum(x, axis=0, keepdims=True)


def zero8():
    return jnp.zeros((8, WIDTH), F32)


def to_row(x4):
    return jnp.concatenate([x4[i : i + 1] for i in range(4)], axis=1)


def put_rows(out_ref, tile_ref, rows):
    tile_ref[...] = jnp.zeros(tile_ref.shape, F32)
    at = 0
    for row in rows:
        for i in range(-(-row.shape[1] // 128)):
            piece = row[:, i * 128 : min((i + 1) * 128, row.shape[1])]
            tile_ref[at : at + 1, 0 : piece.shape[1]] = piece
            at += 1
    out_ref[...] = jnp.broadcast_to(tile_ref[...][None], out_ref.shape)


def norm_of(g, st_ref, q):
    block = st_ref[:, 8 * q : 8 * q + 8, :]
    sums = jnp.sum(block, axis=0)
    mean = sums[0:4] / g.nd
    dev = block[:, 0:4, :] - mean[None]
    spread = sums[4:8] + g.count * jnp.sum(dev * dev, axis=0)
    inv = lax.rsqrt(spread / (g.count * g.nd) + EPS)
    return to_row(mean), to_row(inv)


def sum_of(st_ref, q):
    return to_row(jnp.sum(st_ref[:, 4 * q : 4 * q + 4, :], axis=0))


def back_consts(g, gain, inv, dgain, dshift):
    n = g.count * g.nd
    factor = gain * inv
    return factor, factor * dshift / n, factor * inv * dgain / n


def slope(h, t):
    return 0.5 * ((1.0 + t) + h * (1.0 - t * t))


def local_stats(g, z_ref, masked):
    def one(c, i, kind, seg, r, u):
        x = z_ref[pl.ds(r, 32), :]
        return c + fold(valid(g, kind, x) if masked else x), i

    mean = total(walk(g, one, zero8())) / g.count

    def two(c, i, kind, seg, r, u):
        x = valid(g, kind, z_ref[pl.ds(r, 32), :] - mean)
        return c + fold(x * x), i

    return mean, total(walk(g, two, zero8()))


def dot_rows(rows, most, fn):
    m = chunk_of(rows, most)

    def step(i, c):
        fn(pl.multiple_of(i * m, 16), m)
        return c

    lax.fori_loop(0, rows // m, step, 0)


def dot(a, b):
    return jnp.dot(a, b, preferred_element_type=F32)


def dot_nt(a, b):
    return lax.dot_general(a, b, (((1,), (1,)), ((), ())), preferred_element_type=F32)


def dot_tn(a, b):
    return lax.dot_general(a, b, (((0,), (0,)), ((), ())), preferred_element_type=F32)


def fine(a, b, dims):
    return lax.dot_general(a, b, (dims, ((), ())), precision=HIGHEST, preferred_element_type=F32)


def unpack(flat_ref, wide_ref, mat_ref):
    n = flat_ref.shape[0]
    wide_ref[0:n, :] = flat_ref[...].astype(F32)
    for j in range(4):
        part = wide_ref[pl.ds(j, n // 4, stride=4), :]
        mat_ref[:, j * 128 : (j + 1) * 128] = part.astype(mat_ref.dtype)


def pack(grad, flat_ref):
    n = grad.shape[0]
    for j in range(4):
        flat_ref[pl.ds(j, n, stride=4), :] = grad[:, j * 128 : (j + 1) * 128]


def unpack_group(flat_ref, wide_ref, blocks_ref):
    blocks_ref[...] = jnp.zeros(blocks_ref.shape, BF16)

    def tap(t, c):
        for half in range(2):
            v = flat_ref[pl.ds(pl.multiple_of(t * 256 + half * 128, 128), 128), :].astype(F32)
            wide_ref[pl.ds(0, 128, stride=2), :] = v
            wide_ref[pl.ds(1, 128, stride=2), :] = pltpu.roll(v, 64, 1)
            for q in range(4):
                part = wide_ref[q * 64 : q * 64 + 64, :]
                if q % 2:
                    part = pltpu.roll(part, 64, 1)
                part = part[:, (q % 2) * 64 : (q % 2) * 64 + 64].astype(BF16)
                rows = pl.ds(pl.multiple_of(t * 256, 256) + q * 64, 64)
                blocks_ref[half, rows, q * 64 : q * 64 + 64] = part
        return c

    lax.fori_loop(0, 9, tap, 0)


def pack_group(block, wide_ref, flat_ref, tap, half):
    turned = jnp.transpose(block)
    for q in range(4):
        part = turned[q * 64 : q * 64 + 64, q * 64 : q * 64 + 64]
        wide_ref[q * 64 : q * 64 + 64, 0:64] = part
    even = wide_ref[pl.ds(0, 128, stride=2), :]
    odd = wide_ref[pl.ds(1, 128, stride=2), :]
    row = tap * 256 + half * 128
    flat_ref[row : row + 128, :] = jnp.concatenate([even[:, 0:64], odd[:, 0:64]], axis=1)


def zero_pads(g, ref, index):
    pads = [n * (g.sb + 1) for n in range(g.nb + 1)]
    pads += [g.pad_big + p * (g.ss + 1) for p in range(g.pairs + 1)]
    for unit in pads:
        ref[index, unit * 16 : unit * 16 + 16, :] = jnp.zeros((16, WIDTH), BF16)
    tail = g.pad_units * 16
    if g.urows > tail:
        ref[index, tail : g.urows, :] = jnp.zeros((g.urows - tail, WIDTH), BF16)


def conv_to(g, taps, blocks_ref, nt, into_ref):
    def step(base, m):
        for half in range(2):
            lanes = slice(half * HALF, (half + 1) * HALF)
            acc = None
            for ref, index, off, block in taps:
                window = ref[index, pl.ds(base + off, m), lanes]
                weight = blocks_ref[half, block * HALF : (block + 1) * HALF, :]
                part = dot_nt(window, weight) if nt else dot(window, weight)
                acc = part if acc is None else acc + part
            into_ref[pl.ds(base, m), lanes] = acc

    dot_rows(g.vrows, 820, step)


def turn(g, ref, index, turned_ref):
    def step(i, c):
        part = ref[index, pl.ds(pl.multiple_of(i * 128, 128) + 16, 128), :]
        turned_ref[:, pl.ds(pl.multiple_of(i * 128, 128), 128)] = jnp.transpose(part)
        return c

    lax.fori_loop(0, g.vwide // 128, step, 0)


def group_grad(g, taps, turned_ref, wide_ref, flat_ref):
    for half in range(2):
        lanes = slice(half * HALF, (half + 1) * HALF)
        for ref, index, off, block in taps:
            window = ref[index, off : off + g.vwide, lanes]
            pack_group(dot(turned_ref[lanes, :], window), wide_ref, flat_ref, block, half)


def back_v(u):
    return pl.multiple_of(u - 16, 16)


def put_wide(wide_ref, rows, x):
    wide_ref[0, rows, :] = x[:, 0:128]
    wide_ref[1, rows, 0 : C_IN - 128] = x[:, 128:C_IN]


def get_wide(wide_ref, rows):
    return jnp.concatenate([wide_ref[0, rows, :], wide_ref[1, rows, :][:, 0 : C_IN - 128]], axis=1)


def split_kernel(g, big_ref, small_ref, xp_ref, wide_ref):
    wide_ref[...] = jnp.zeros(wide_ref.shape, F32)

    def big(n, c):
        def load(k, c):
            put_wide(wide_ref, pl.ds(pl.multiple_of(k * 32, 32), 2 * g.sb), big_ref[n, k].astype(F32))
            return c

        lax.fori_loop(0, 2 * g.sb, load, 0)

        def split(h, c):
            r = pl.multiple_of((n * g.sb + h) * 16, 16)
            for a in range(2):
                for b in range(2):
                    part = get_wide(wide_ref, pl.ds((2 * h + a) * 32 + b, 16, stride=2))
                    xp_ref[2 * a + b, pl.ds(r, 16), :] = part.astype(BF16)
            return c

        return lax.fori_loop(0, g.sb, split, c)

    lax.fori_loop(0, g.nb, big, 0)
    wide_ref[...] = jnp.zeros(wide_ref.shape, F32)

    def small(p, c):
        def load(k, c):
            for q in range(2):
                at = pl.multiple_of((q * 2 * g.ss + k) * 16, 16)
                put_wide(wide_ref, pl.ds(at, 2 * g.ss), small_ref[2 * p + q, k].astype(F32))
            return c

        lax.fori_loop(0, 2 * g.ss, load, 0)

        def split(h, c):
            r = pl.multiple_of((g.units_big + p * g.ss + h) * 16, 16)
            for a in range(2):
                for b in range(2):
                    parts = [
                        get_wide(wide_ref, pl.ds((q * 2 * g.ss + 2 * h + a) * 16 + b, 8, stride=2))
                        for q in range(2)
                    ]
                    xp_ref[2 * a + b, pl.ds(r, 16), :] = jnp.concatenate(parts, 0).astype(BF16)
            return c

        return lax.fori_loop(0, g.ss, split, c)

    lax.fori_loop(0, g.pairs, small, 0)


def enter_kernel(g, xp_ref, ef_ref, sf_ref, st_ref, we_ref, ws_ref, wide_ref, z_ref, tile_ref):
    unpack(ef_ref, wide_ref, we_ref)
    unpack(sf_ref, wide_ref, ws_ref)
    ones = jnp.ones((8, g.rows), BF16)
    sums = [dot(ones, xp_ref[ph])[0:1] for ph in range(4)]
    count_in = 4 * g.count
    mean_x = (sums[0] + sums[1] + sums[2] + sums[3]) / count_in
    dims = ((1,), (0,))
    mean = fine(mean_x, we_ref[...].astype(F32), dims)

    def phase(ph, acc):
        def mm(base, m):
            z_ref[pl.ds(base, m), :] = dot(xp_ref[ph, pl.ds(base, m), :], we_ref[...])

        dot_rows(g.rows, 740, mm)

        def two(c, i, kind, seg, r, u):
            x = valid(g, kind, z_ref[pl.ds(r, 32), :] - mean)
            return c + fold(x * x), i

        return walk(g, two, acc)

    spread = total(lax.fori_loop(0, 4, phase, zero8()))

    def mm(base, m):
        z_ref[pl.ds(base, m), :] = dot(xp_ref[0, pl.ds(base, m), :], ws_ref[...])

    dot_rows(g.rows, 740, mm)
    skip_mean, skip_spread = local_stats(g, z_ref, False)
    put_rows(st_ref, tile_ref, [mean, spread / 4, skip_mean, skip_spread])


def acts_pass(g, ph, z_ref, m, sg, sh, acts_ref, slots, slope_ref=None):
    def act(c, i, kind, seg, r, u):
        h = (z_ref[pl.ds(r, 32), :] - m) * sg + sh
        t = jnp.tanh(h)
        a = valid(g, kind, h + h * t)
        for slot, shift in slots:
            moved = pltpu.roll(a, shift % 32, 0) if shift else a
            acts_ref[slot, pl.ds(u, 32), :] = moved.astype(BF16)
        if slope_ref is not None:
            slope_ref[pl.ds(r, 32), :] = slope(h, t)
        return c, i

    walk(g, act, jnp.int32(0))


def compress(g, v_ref, out_ref):
    def one(c, i, kind, seg, r, u):
        x = v_ref[pl.ds(back_v(u), 32), :]
        out_ref[pl.ds(r, 32), :] = x
        return c + fold(valid(g, kind, x)), i

    mean = total(walk(g, one, zero8())) / g.count

    def two(c, i, kind, seg, r, u):
        x = valid(g, kind, out_ref[pl.ds(r, 32), :] - mean)
        return c + fold(x * x), i

    return mean, total(walk(g, two, zero8()))


SLOTS = (((0, 0),), ((1, 0), (2, 1)), ((3, 0),), ((4, 0), (5, 1)))


def first_taps(ref):
    taps = []
    for tap in range(9):
        r, c = divmod(tap, 3)
        slot = (3 if r != 1 else 0) + (2, 0, 1)[c]
        taps.append((ref, slot, 0 if r == 0 else 16, tap))
    return taps


def second_taps(ref):
    return [(ref, tap % 3, 16 * (tap // 3), tap) for tap in range(9)]


def conv_one_kernel(
    g, xp_ref, we_ref, st_ref, gf_ref, gain_ref, bias_ref, g1_ref, sto_ref, bd_ref, acts_ref, z_ref,
    v_ref, wide_ref, tile_ref
):
    unpack_group(gf_ref, wide_ref, bd_ref)
    m, inv = norm_of_one(g, st_ref)
    sg = 0.5 * inv * gain_ref[...]
    sh = 0.5 * bias_ref[...]
    for slot in range(6):
        zero_pads(g, acts_ref, slot)
    for ph in range(4):

        def mm(base, rows, ph=ph):
            z_ref[pl.ds(base, rows), :] = dot(xp_ref[ph, pl.ds(base, rows), :], we_ref[...])

        dot_rows(g.rows, 740, mm)
        acts_pass(g, ph, z_ref, m, sg, sh, acts_ref, SLOTS[ph])
    conv_to(g, first_taps(acts_ref), bd_ref, False, v_ref)
    mean, spread = compress(g, v_ref, g1_ref)
    put_rows(sto_ref, tile_ref, [mean, spread])


def norm_of_one(g, st_ref):
    return norm_of(g, st_ref, 0)


def conv_two_kernel(
    g, e_ref, st_ref, gf_ref, gain_ref, bias_ref, g2_ref, sto_ref, bd_ref, acts_ref, v_ref, wide_ref,
    tile_ref
):
    unpack_group(gf_ref, wide_ref, bd_ref)
    m, inv = norm_of(g, st_ref, 0)
    for slot in range(3):
        zero_pads(g, acts_ref, slot)
    slots = ((0, 1), (1, 0), (2, -1))
    acts_pass(g, 0, e_ref, m, 0.5 * inv * gain_ref[...], 0.5 * bias_ref[...], acts_ref, slots)
    conv_to(g, second_taps(acts_ref), bd_ref, False, v_ref)
    mean, spread = compress(g, v_ref, g2_ref)
    put_rows(sto_ref, tile_ref, [mean, spread])


def pools(g, fn, pool_ref):
    def inner(kind):
        return (zero8(), zero8()) if kind else zero8()

    def step(c, acc, kind, seg, r, u):
        x = fn(kind, seg, r, u)
        if kind:
            return c, (acc[0] + x[0:8] + x[16:24], acc[1] + x[8:16] + x[24:32])
        return c, acc + fold(x)

    def done(kind, seg, c, acc):
        if kind:
            pool_ref[pl.ds(g.nb + 2 * seg, 1), :] = total(acc[0])
            pool_ref[pl.ds(g.nb + 2 * seg + 1, 1), :] = total(acc[1])
        else:
            pool_ref[pl.ds(seg, 1), :] = total(acc)
        return c

    walk(g, step, jnp.int32(0), inner, done)


def spread_rows(g, ref, kind, seg):
    if kind:
        one = jnp.broadcast_to(ref[pl.ds(g.nb + 2 * seg, 1), :], (8, WIDTH))
        two = jnp.broadcast_to(ref[pl.ds(g.nb + 2 * seg + 1, 1), :], (8, WIDTH))
        return jnp.concatenate([one, two, one, two], axis=0)
    return jnp.broadcast_to(ref[pl.ds(seg, 1), :], (32, WIDTH))


def per_pixel(g):
    row = lax.broadcasted_iota(jnp.int32, (g.crops, 1), 0)
    return jnp.where(row < g.nb, 1.0 / g.sb**2, 1.0 / g.ss**2)


def sigmoid(x):
    return 0.5 * jnp.tanh(0.5 * x) + 0.5


def squeeze(pool, down, dbias, up, ubias):
    u = fine(pool, down, ((1,), (0,))) + dbias
    q = u * sigmoid(u)
    return u, q, sigmoid(fine(q, up, ((1,), (0,))) + ubias)


def leave_kernel(
    g, g_ref, st_ref, down_ref, db_ref, uf_ref, ub_ref, lf_ref, gain_ref, bias_ref,
    z_ref, sto_ref, pool_ref, gate_ref, up_ref, wl_ref, mid_ref, sc_ref, wide_ref, tile_ref
):
    unpack(uf_ref, wide_ref, up_ref)
    unpack(lf_ref, wide_ref, wl_ref)
    m, inv = norm_of(g, st_ref, 0)
    sg = 0.5 * inv * gain_ref[...]
    sh = 0.5 * bias_ref[...]

    def act(kind, seg, r, u):
        h = (g_ref[pl.ds(r, 32), :] - m) * sg + sh
        a = valid(g, kind, h + h * jnp.tanh(h))
        mid_ref[pl.ds(r, 32), :] = a
        return a

    pools(g, act, pool_ref)
    pool_ref[...] = pool_ref[...] * per_pixel(g)
    unused, unused, gate = squeeze(
        pool_ref[...], down_ref[...].astype(F32), db_ref[...], up_ref[...].astype(F32), ub_ref[...]
    )
    gate_ref[...] = gate

    def scale(c, i, kind, seg, r, u):
        x = mid_ref[pl.ds(r, 32), :] * spread_rows(g, gate_ref, kind, seg)
        sc_ref[pl.ds(r, 32), :] = x.astype(BF16)
        return c, i

    walk(g, scale, jnp.int32(0))

    def mm(base, rows):
        z_ref[pl.ds(base, rows), :] = dot(sc_ref[pl.ds(base, rows), :], wl_ref[...])

    dot_rows(g.rows, 740, mm)
    mean, spread = local_stats(g, z_ref, False)
    put_rows(sto_ref, tile_ref, [mean, spread])


def skip_product(g, xp_ref, ws_ref, s_ref):
    def mm(base, rows):
        s_ref[pl.ds(base, rows), :] = dot(xp_ref[0, pl.ds(base, rows), :], ws_ref[...])

    dot_rows(g.rows, 740, mm)


def middle_kernel(
    g, z_ref, xp_ref, ws_ref, st1_ref, st3_ref, lg_ref, lb_ref, sg_ref, sb_ref, ef_ref,
    mid_ref, e_ref, sto_ref, we_ref, s_ref, low_ref, wide_ref, tile_ref
):
    unpack(ef_ref, wide_ref, we_ref)
    skip_product(g, xp_ref, ws_ref, s_ref)
    ms, invs = norm_of(g, st1_ref, 1)
    ml, invl = norm_of(g, st3_ref, 0)
    al = 0.5 * invl * lg_ref[...]
    a_s = 0.5 * invs * sg_ref[...]
    sh = 0.5 * (lb_ref[...] + sb_ref[...])

    def act(c, i, kind, seg, r, u):
        h = (z_ref[pl.ds(r, 32), :] - ml) * al + (s_ref[pl.ds(r, 32), :] - ms) * a_s + sh
        a = valid(g, kind, h + h * jnp.tanh(h))
        mid_ref[pl.ds(r, 32), :] = a
        low_ref[pl.ds(r, 32), :] = a.astype(BF16)
        return c, i

    walk(g, act, jnp.int32(0))

    def mm(base, rows):
        e_ref[pl.ds(base, rows), :] = dot(low_ref[pl.ds(base, rows), :], we_ref[...])

    dot_rows(g.rows, 740, mm)
    mean, spread = local_stats(g, e_ref, False)
    put_rows(sto_ref, tile_ref, [mean, spread])


def final_kernel(
    g, z_ref, mid_ref, st_ref, gain_ref, bias_ref, bc_ref, sc_ref, bo_ref, so_ref, ds_ref, sto_ref,
    cot_ref, tile_ref
):
    m, inv = norm_of(g, st_ref, 0)
    sg = 0.5 * inv * gain_ref[...]
    sh = 0.5 * bias_ref[...]
    cot_ref[...] = jnp.zeros(cot_ref.shape, F32)

    def load_big(n, c):
        def row(k, c):
            r = pl.multiple_of((n * g.sb + k) * 16, 16)
            cot_ref[pl.ds(r, g.sb), :] = bc_ref[n, k].astype(F32)
            return c

        return lax.fori_loop(0, g.sb, row, c)

    def load_small(p, c):
        def row(k, c):
            r = pl.multiple_of((g.units_big + p * g.ss + k) * 16, 16)
            for q in range(2):
                at = pl.multiple_of(r + q * 8, 8)
                cot_ref[pl.ds(at, g.ss), :] = sc_ref[2 * p + q, k].astype(F32)
            return c

        return lax.fori_loop(0, g.ss, row, c)

    lax.fori_loop(0, g.nb, load_big, 0)
    lax.fori_loop(0, g.pairs, load_small, 0)

    def act(c, i, kind, seg, r, u):
        dev = z_ref[pl.ds(r, 32), :] - m
        h = dev * sg + (sh + 0.5 * mid_ref[pl.ds(r, 32), :])
        t = jnp.tanh(h)
        out = h + h * t
        k = lax.div(r, 16) - (g.units_big + seg * g.ss if kind else seg * g.sb)
        for j in range(2):
            part = out[16 * j : 16 * j + 16]
            if kind:
                so_ref[2 * seg, k + j] = part[0 : g.ss].astype(BF16)
                so_ref[2 * seg + 1, k + j] = part[8 : 8 + g.ss].astype(BF16)
            else:
                bo_ref[seg, k + j] = part[0 : g.sb].astype(BF16)
        d = cot_ref[pl.ds(r, 32), :] * slope(h, t)
        ds_ref[pl.ds(r, 32), :] = d
        return (c[0] + fold(d), c[1] + fold(d * dev)), i

    shift, gain = walk(g, act, (zero8(), zero8()))
    put_rows(sto_ref, tile_ref, [total(shift), total(gain) * inv])


def squeeze_back(pool, gate, dgate, down, dbias, up, ubias, per):
    u, q, unused = squeeze(pool, down, dbias, up, ubias)
    dv = dgate * gate * (1.0 - gate)
    dup = fine(q, dv, ((0,), (0,)))
    dub = total(dv)
    dq = fine(dv, up, ((1,), (1,)))
    s = sigmoid(u)
    du = dq * (s * (1.0 + u * (1.0 - s)))
    ddown = fine(pool, du, ((0,), (0,)))
    ddb = total(du)
    dpool = fine(du, down, ((1,), (1,))) * per
    return dup, dub, ddown, ddb, dpool


def gate_back(
    g, dl_ref, wl_ref, g_ref, stg_ref, ggain_ref, gbias_ref, pool_ref, gate_ref, down_ref, db_ref,
    up_ref, ub_ref, dy_ref, dleave_ref, ddown_ref, dup_ref, mid_ref, sl_ref, sc_ref, dsc_ref,
    dg_ref, dp_ref
):
    mg, invg = norm_of(g, stg_ref, 0)
    ag = 0.5 * invg * ggain_ref[...]
    sh = 0.5 * gbias_ref[...]

    def mm(base, rows):
        dsc_ref[pl.ds(base, rows), :] = dot_nt(dl_ref[pl.ds(base, rows), :], wl_ref[...])

    dot_rows(g.rows, 740, mm)

    def act(kind, seg, r, u):
        h = (g_ref[pl.ds(r, 32), :] - mg) * ag + sh
        t = jnp.tanh(h)
        a = valid(g, kind, h + h * t)
        mid_ref[pl.ds(r, 32), :] = a
        sl_ref[pl.ds(r, 32), :] = slope(h, t)
        sc_ref[pl.ds(r, 32), :] = (a * spread_rows(g, gate_ref, kind, seg)).astype(BF16)
        return a * dsc_ref[pl.ds(r, 32), :]

    pools(g, act, dg_ref)
    pack(dot_tn(sc_ref[...], dl_ref[...]), dleave_ref)
    dup, dub, ddown, ddb, dpool = squeeze_back(
        pool_ref[...], gate_ref[...], dg_ref[...], down_ref[...].astype(F32), db_ref[...],
        up_ref[...].astype(F32), ub_ref[...], per_pixel(g)
    )
    pack(dup, dup_ref)
    ddown_ref[...] = ddown
    dp_ref[...] = dpool

    def act_back(c, i, kind, seg, r, u):
        d = dsc_ref[pl.ds(r, 32), :] * spread_rows(g, gate_ref, kind, seg)
        d = valid(g, kind, (d + spread_rows(g, dp_ref, kind, seg)) * sl_ref[pl.ds(r, 32), :])
        dy_ref[pl.ds(r, 32), :] = d
        dev = g_ref[pl.ds(r, 32), :] - mg
        return (c[0] + fold(d), c[1] + fold(d * dev)), i

    shift, gain = walk(g, act_back, (zero8(), zero8()))
    return total(shift), total(gain) * invg, dub, ddb


def norm_back_pass(g, dy_ref, z_ref, m, consts, out_ref):
    f, c0, c1 = consts

    def one(c, i, kind, seg, r, u):
        x = f * dy_ref[pl.ds(r, 32), :] - c0 - (z_ref[pl.ds(r, 32), :] - m) * c1
        out_ref[pl.ds(r, 32), :] = valid(g, kind, x).astype(BF16)
        return c, i

    walk(g, one, jnp.int32(0))


def leave_two_back_kernel(
    g, z_ref, ds_ref, stz_ref, sts_ref, lgain_ref, g_ref, stg_ref, ggain_ref, gbias_ref, pool_ref,
    gate_ref, down_ref, db_ref, up_ref, ub_ref, wl_ref,
    dy_ref, sto_ref, dleave_ref, ddown_ref, dup_ref, dlg_ref, dlb_ref,
    dl_ref, mid_ref, sl_ref, sc_ref, dsc_ref, dg_ref, dp_ref, tile_ref
):
    m, inv = norm_of(g, stz_ref, 0)
    dshift, dgain = sum_of(sts_ref, 0), sum_of(sts_ref, 1)
    dlb_ref[...] = dshift
    dlg_ref[...] = dgain
    norm_back_pass(g, ds_ref, z_ref, m, back_consts(g, lgain_ref[...], inv, dgain, dshift), dl_ref)
    rows = gate_back(
        g, dl_ref, wl_ref, g_ref, stg_ref, ggain_ref, gbias_ref, pool_ref, gate_ref, down_ref,
        db_ref, up_ref, ub_ref, dy_ref, dleave_ref, ddown_ref, dup_ref, mid_ref, sl_ref, sc_ref,
        dsc_ref, dg_ref, dp_ref
    )
    put_rows(sto_ref, tile_ref, rows)


def bias_sums(st_ref, wide, db_out, ub_out):
    ub_out[...] = sum_of(st_ref, 2)
    db_out[...] = jnp.sum(st_ref[:, 12:13, :], axis=0)[:, 0:wide]


def conv_two_back_kernel(
    g, dy_ref, g_ref, stg_ref, sts_ref, ggain_ref, e_ref, ste_ref, egain_ref, ebias_ref, bd_ref,
    dye_ref, sto_ref, dgroup_ref, dgg_ref, dgb_ref, ddb_ref, dub_ref,
    acts_ref, dz_ref, turned_ref, v_ref, sl_ref, wide_ref, tile_ref
):
    m, inv = norm_of(g, stg_ref, 0)
    dshift, dgain = sum_of(sts_ref, 0), sum_of(sts_ref, 1)
    dgb_ref[...] = dshift
    dgg_ref[...] = dgain
    bias_sums(sts_ref, ddb_ref.shape[1], ddb_ref, dub_ref)
    f, c0, c1 = back_consts(g, ggain_ref[...], inv, dgain, dshift)
    for slot in range(3):
        zero_pads(g, acts_ref, slot)
        zero_pads(g, dz_ref, slot)

    def one(c, i, kind, seg, r, u):
        x = f * dy_ref[pl.ds(r, 32), :] - c0 - (g_ref[pl.ds(r, 32), :] - m) * c1
        x = valid(g, kind, x)
        for slot, shift in ((0, 1), (1, 0), (2, -1)):
            moved = pltpu.roll(x, shift % 32, 0) if shift else x
            dz_ref[slot, pl.ds(u, 32), :] = moved.astype(BF16)
        return c, i

    walk(g, one, jnp.int32(0))
    taps = [(dz_ref, 2 - tap % 3, 16 * (2 - tap // 3), tap) for tap in range(9)]
    conv_to(g, taps, bd_ref, True, v_ref)
    me, inve = norm_of(g, ste_ref, 0)
    slots = ((0, 1), (1, 0), (2, -1))
    sg = 0.5 * inve * egain_ref[...]
    acts_pass(g, 0, e_ref, me, sg, 0.5 * ebias_ref[...], acts_ref, slots, sl_ref)
    turn(g, dz_ref, 1, turned_ref)
    group_grad(g, second_taps(acts_ref), turned_ref, wide_ref, dgroup_ref)

    def back(c, i, kind, seg, r, u):
        d = valid(g, kind, v_ref[pl.ds(back_v(u), 32), :] * sl_ref[pl.ds(r, 32), :])
        dye_ref[pl.ds(r, 32), :] = d
        return (c[0] + fold(d), c[1] + fold(d * (e_ref[pl.ds(r, 32), :] - me))), i

    shift, gain = walk(g, back, (zero8(), zero8()))
    put_rows(sto_ref, tile_ref, [total(shift), total(gain) * inve])


def enter_two_back_kernel(
    g, dye_ref, e_ref, ste_ref, sts_ref, egain_ref, mid_ref, ds_ref, we_ref, z_ref, st3_ref, xp_ref,
    ws_ref, st1_ref, lg_ref, lb_ref, sg_ref, sb_ref,
    d1_ref, sto_ref, denter_ref, deg_ref, deb_ref, de_ref, low_ref, s_ref, dm_ref, tile_ref
):
    m, inv = norm_of(g, ste_ref, 0)
    dshift, dgain = sum_of(sts_ref, 0), sum_of(sts_ref, 1)
    deb_ref[...] = dshift
    deg_ref[...] = dgain
    norm_back_pass(g, dye_ref, e_ref, m, back_consts(g, egain_ref[...], inv, dgain, dshift), de_ref)
    low_ref[...] = mid_ref[...].astype(BF16)

    def mm(base, rows):
        dm_ref[pl.ds(base, rows), :] = dot_nt(de_ref[pl.ds(base, rows), :], we_ref[...])

    dot_rows(g.rows, 740, mm)
    pack(dot_tn(low_ref[...], de_ref[...]), denter_ref)
    skip_product(g, xp_ref, ws_ref, s_ref)
    ms, invs = norm_of(g, st1_ref, 1)
    ml, invl = norm_of(g, st3_ref, 0)
    al = 0.5 * invl * lg_ref[...]
    a_s = 0.5 * invs * sg_ref[...]
    sh = 0.5 * (lb_ref[...] + sb_ref[...])

    def act(c, i, kind, seg, r, u):
        dev = z_ref[pl.ds(r, 32), :] - ml
        devs = s_ref[pl.ds(r, 32), :] - ms
        h = dev * al + devs * a_s + sh
        d = (ds_ref[pl.ds(r, 32), :] + dm_ref[pl.ds(r, 32), :]) * slope(h, jnp.tanh(h))
        d1_ref[pl.ds(r, 32), :] = d
        return (c[0] + fold(d), c[1] + fold(d * dev), c[2] + fold(d * devs)), i

    shift, gain, gains = walk(g, act, (zero8(), zero8(), zero8()))
    put_rows(sto_ref, tile_ref, [total(shift), total(gain) * invl, total(gains) * invs])


def leave_one_back_kernel(
    g, d1_ref, z_ref, st3_ref, xp_ref, ws_ref, st1_ref, sts_ref, lgain_ref, sgain_ref,
    g_ref, stg_ref, ggain_ref, gbias_ref, pool_ref, gate_ref, down_ref, db_ref, up_ref, ub_ref,
    wl_ref,
    dy_ref, sto_ref, dsk_ref, dleave_ref, dshort_ref, ddown_ref, dup_ref, dlg_ref, dlb_ref, dsg_ref,
    dl_ref, s_ref, mid_ref, sl_ref, sc_ref, dsc_ref, dg_ref, dp_ref, tile_ref
):
    m, inv = norm_of(g, st3_ref, 0)
    ms, invs = norm_of(g, st1_ref, 1)
    dshift, dgain, dgains = sum_of(sts_ref, 0), sum_of(sts_ref, 1), sum_of(sts_ref, 2)
    dlb_ref[...] = dshift
    dlg_ref[...] = dgain
    dsg_ref[...] = dgains
    skip_product(g, xp_ref, ws_ref, s_ref)
    norm_back_pass(g, d1_ref, z_ref, m, back_consts(g, lgain_ref[...], inv, dgain, dshift), dl_ref)
    norm_back_pass(
        g, d1_ref, s_ref, ms, back_consts(g, sgain_ref[...], invs, dgains, dshift), dsk_ref
    )
    pack(dot_tn(xp_ref[0], dsk_ref[...]), dshort_ref)
    rows = gate_back(
        g, dl_ref, wl_ref, g_ref, stg_ref, ggain_ref, gbias_ref, pool_ref, gate_ref, down_ref,
        db_ref, up_ref, ub_ref, dy_ref, dleave_ref, ddown_ref, dup_ref, mid_ref, sl_ref, sc_ref,
        dsc_ref, dg_ref, dp_ref
    )
    put_rows(sto_ref, tile_ref, rows)


def conv_one_back_kernel(
    g, dy_ref, g_ref, stg_ref, sts_ref, ggain_ref, xp_ref, we_ref, ste_ref, egain_ref, ebias_ref,
    bd_ref, dye_ref, sto_ref, dgroup_ref, dgg_ref, dgb_ref, ddb_ref, dub_ref,
    acts_ref, dz_ref, turned_ref, v_ref, z_ref, sl_ref, wide_ref, tile_ref
):
    m, inv = norm_of(g, stg_ref, 0)
    dshift, dgain = sum_of(sts_ref, 0), sum_of(sts_ref, 1)
    dgb_ref[...] = dshift
    dgg_ref[...] = dgain
    bias_sums(sts_ref, ddb_ref.shape[1], ddb_ref, dub_ref)
    f, c0, c1 = back_consts(g, ggain_ref[...], inv, dgain, dshift)
    for slot in range(6):
        zero_pads(g, acts_ref, slot)
    for slot in range(2):
        zero_pads(g, dz_ref, slot)

    def one(c, i, kind, seg, r, u):
        x = f * dy_ref[pl.ds(r, 32), :] - c0 - (g_ref[pl.ds(r, 32), :] - m) * c1
        x = valid(g, kind, x)
        dz_ref[0, pl.ds(u, 32), :] = x.astype(BF16)
        dz_ref[1, pl.ds(u, 32), :] = pltpu.roll(x, 31, 0).astype(BF16)
        return c, i

    walk(g, one, jnp.int32(0))
    me, inve = norm_of_one(g, ste_ref)
    sg = 0.5 * inve * egain_ref[...]
    sh = 0.5 * ebias_ref[...]
    sums = (zero8(), zero8())
    for ph in range(4):

        def mm(base, rows, ph=ph):
            z_ref[pl.ds(base, rows), :] = dot(xp_ref[ph, pl.ds(base, rows), :], we_ref[...])

        dot_rows(g.rows, 740, mm)
        acts_pass(g, ph, z_ref, me, sg, sh, acts_ref, SLOTS[ph], sl_ref)
        rows_of = ((2, 16), (0, 32)) if ph // 2 else ((1, 16),)
        cols_of = ((2, 0), (0, 1)) if ph % 2 else ((1, 0),)
        taps = [(dz_ref, slot, off, 3 * r + c) for r, off in rows_of for c, slot in cols_of]
        conv_to(g, taps, bd_ref, True, v_ref)

        def back(c, i, kind, seg, r, u, ph=ph):
            d = valid(g, kind, v_ref[pl.ds(back_v(u), 32), :] * sl_ref[pl.ds(r, 32), :])
            dye_ref[ph, pl.ds(r, 32), :] = d.astype(dye_ref.dtype)
            return (c[0] + fold(d), c[1] + fold(d * (z_ref[pl.ds(r, 32), :] - me))), i

        sums = walk(g, back, sums)
    turn(g, dz_ref, 0, turned_ref)
    group_grad(g, first_taps(acts_ref), turned_ref, wide_ref, dgroup_ref)
    put_rows(sto_ref, tile_ref, [total(sums[0]), total(sums[1]) * inve])


def enter_one_back_kernel(
    g, dye_ref, xp_ref, we_ref, ste_ref, sts_ref, egain_ref, dsk_ref, ws_ref,
    dbig_ref, dsmall_ref, denter_ref, deg_ref, deb_ref, z_ref, de_ref, dx_ref, wide_ref
):
    me, inve = norm_of_one(g, ste_ref)
    dshift, dgain = sum_of(sts_ref, 0), sum_of(sts_ref, 1)
    deb_ref[...] = dshift
    deg_ref[...] = dgain
    n = 4 * g.count * g.nd
    f = egain_ref[...] * inve
    c0, c1 = f * dshift / n, f * inve * dgain / n
    grad = None
    for ph in range(4):

        def mm(base, rows, ph=ph):
            z_ref[pl.ds(base, rows), :] = dot(xp_ref[ph, pl.ds(base, rows), :], we_ref[...])

        dot_rows(g.rows, 740, mm)

        def one(c, i, kind, seg, r, u, ph=ph):
            x = f * dye_ref[ph, pl.ds(r, 32), :].astype(F32) - c0 - (z_ref[pl.ds(r, 32), :] - me) * c1
            de_ref[pl.ds(r, 32), :] = valid(g, kind, x).astype(BF16)
            return c, i

        walk(g, one, jnp.int32(0))

        def down(base, rows, ph=ph):
            x = dot_nt(de_ref[pl.ds(base, rows), :], we_ref[...])
            if ph == 0:
                x = x + dot_nt(dsk_ref[pl.ds(base, rows), :], ws_ref[...])
            dx_ref[ph, pl.ds(base, rows), :] = x

        dot_rows(g.rows, 740, down)
        part = dot_tn(xp_ref[ph], de_ref[...])
        grad = part if grad is None else grad + part
    pack(grad, denter_ref)

    def big(n, c):
        def row(h, c):
            r = pl.multiple_of((n * g.sb + h) * 16, 16)
            for a in range(2):
                put_wide(wide_ref, pl.ds(0, 16, stride=2), dx_ref[2 * a, pl.ds(r, 16), :])
                put_wide(wide_ref, pl.ds(1, 16, stride=2), dx_ref[2 * a + 1, pl.ds(r, 16), :])
                dbig_ref[n, 2 * h + a] = get_wide(wide_ref, slice(0, 2 * g.sb)).astype(BF16)
            return c

        return lax.fori_loop(0, g.sb, row, c)

    def small(p, c):
        def row(h, c):
            r = pl.multiple_of((g.units_big + p * g.ss + h) * 16, 16)
            for a in range(2):
                put_wide(wide_ref, pl.ds(0, 16, stride=2), dx_ref[2 * a, pl.ds(r, 16), :])
                put_wide(wide_ref, pl.ds(1, 16, stride=2), dx_ref[2 * a + 1, pl.ds(r, 16), :])
                dsmall_ref[2 * p, 2 * h + a] = get_wide(wide_ref, slice(0, 2 * g.ss)).astype(BF16)
                dsmall_ref[2 * p + 1, 2 * h + a] = get_wide(wide_ref, slice(16, 16 + 2 * g.ss)).astype(BF16)
            return c

        return lax.fori_loop(0, g.ss, row, c)

    lax.fori_loop(0, g.nb, big, 0)
    lax.fori_loop(0, g.pairs, small, 0)


def held(shape, dtype):
    lanes = -(-shape[-1] // 128) * 128
    rows = -(-shape[-2] // 16) * 16
    lead = 1
    for n in shape[:-2]:
        lead *= n
    return lead * rows * lanes * jnp.dtype(dtype).itemsize


def call(kernel, micros, outs, scratch, *args):
    sizes = [held(a.shape, a.dtype) for a in args] + [held(*o) for o in outs + scratch]
    return pl.pallas_call(
        kernel,
        out_shape=[jax.ShapeDtypeStruct(shape, dtype) for shape, dtype in outs],
        in_specs=[pl.BlockSpec(memory_space=pltpu.VMEM)] * len(args),
        out_specs=[pl.BlockSpec(memory_space=pltpu.VMEM)] * len(outs),
        scratch_shapes=[pltpu.VMEM(shape, dtype) for shape, dtype in scratch],
        compiler_params=pltpu.CompilerParams(
            vmem_limit_bytes=min(VMEM_BYTES, sum(sizes) + SLACK_BYTES)
        ),
        cost_estimate=pl.CostEstimate(
            flops=int(micros * 1e9), bytes_accessed=int(micros * 1e6), transcendentals=0
        ),
    )(*args)


def exchange(rows):
    return lax.all_to_all(rows, AXES, 0, 0)


def gather_flat(members):
    if all(m.shape[0] % 128 == 0 for m in members):
        rows = [m.shape[0] // 128 for m in members]
        packed = jnp.concatenate([m.reshape(-1, 128) for m in members], axis=0)
        whole = lax.all_gather(packed, AXES, axis=0, tiled=False)
        at, result = 0, []
        for count in rows:
            result.append(whole[:, at : at + count].reshape(-1, 128))
            at += count
        return result
    return [lax.all_gather(m, AXES, axis=0, tiled=True).reshape(-1, 128) for m in members]


def gather_first(nd, members):
    if all(m.shape[0] % 128 == 0 for m in members):
        rows = [m.shape[0] // 128 for m in members]
        packed = jnp.concatenate([m.reshape(-1, 128) for m in members], axis=0)
        whole = exchange(jnp.broadcast_to(packed[None], (nd,) + packed.shape))
        at, result = 0, []
        for count in rows:
            result.append(whole[:, at : at + count].reshape(-1, 128))
            at += count
        return result
    return gather_flat(members)


def scatter_sums(nd, grads):
    sizes = [g.size // nd for g in grads]
    packed = jnp.concatenate([g.reshape(nd, -1).astype(BF16) for g in grads], axis=1)
    width = packed.shape[1]
    if width % 128 == 0:
        packed = packed.reshape(nd, width // 128, 128)
    got = lax.all_to_all(packed, AXES, 0, 0)
    summed = jnp.sum(got.astype(F32), axis=0).reshape(-1)
    at, result = 0, []
    for size in sizes:
        result.append(summed[at : at + size])
        at += size
    return result


def per_device(
    big_crops, small_crops, big_cot, small_cot,
    enter_one, engain_one, enbias_one, group_one, grgain_one, grbias_one,
    sqdown_one, sqdbias_one, squp_one, squbias_one, leave_one, lvgain_one, lvbias_one,
    shortcut_one, scgain_one, scbias_one,
    enter_two, engain_two, enbias_two, group_two, grgain_two, grbias_two,
    sqdown_two, sqdbias_two, squp_two, squbias_two, leave_two, lvgain_two, lvbias_two,
):
    nd = lax.axis_size(AXES)
    g = Lay(nd, big_crops.shape[0], small_crops.shape[0], big_cot.shape[1], small_cot.shape[1])
    row = lambda v: v.reshape(1, -1)
    kern = lambda f: functools.partial(f, g)
    big_f = ((g.rows, WIDTH), F32)
    big_b = ((g.rows, WIDTH), BF16)
    st8 = ((nd, 8, 128), F32)
    st16 = ((nd, 16, 128), F32)
    tile8 = ((8, 128), F32)
    tile16 = ((16, 128), F32)
    one_row = ((1, WIDTH), F32)
    square = ((WIDTH, WIDTH), BF16)
    wide = ((4 * WIDTH, 128), F32)
    slab = (g.urows, WIDTH)
    vbuf = ((g.vrows, WIDTH), F32)
    blocks = ((2, 9 * HALF, HALF), BF16)
    wide_g = ((HALF, 128), F32)

    enter_f, short_f = gather_first(nd, [enter_one, shortcut_one])
    (group_f,) = gather_first(nd, [group_one])
    leave_f, down_f, up_f = gather_first(nd, [leave_one, sqdown_one, squp_one])
    enter2_f, group2_f, leave2_f, down2, up2_f = gather_flat(
        [enter_two, group_two, leave_two, sqdown_two, squp_two]
    )
    down1 = down_f.reshape(WIDTH, SE_ONE)

    (xp,) = call(
        kern(split_kernel), 6, [((4, g.rows, C_IN), BF16)], [((2, 2 * g.sb * 32, 128), F32)],
        big_crops, small_crops,
    )
    st1, we1, ws1 = call(
        kern(enter_kernel), 11, [st16, ((C_IN, WIDTH), BF16), ((C_IN, WIDTH), BF16)],
        [wide, big_f, tile16], xp, enter_f, short_f,
    )
    st1 = exchange(st1)
    g1, st2, bd1 = call(
        kern(conv_one_kernel), 20, [big_f, st8, blocks],
        [((6,) + slab, BF16), big_f, vbuf, wide_g, tile8],
        xp, we1, st1, group_f, row(engain_one), row(enbias_one),
    )
    st2 = exchange(st2)
    pool_f = ((g.crops, WIDTH), F32)
    z1, st3, pool1, gate1, up1, wl1 = call(
        kern(leave_kernel), 9,
        [big_f, st8, pool_f, pool_f, ((SE_ONE, WIDTH), BF16), square],
        [big_f, big_b, wide, tile8],
        g1, st2, down1, row(sqdbias_one), up_f, row(squbias_one), leave_f, row(grgain_one), row(grbias_one),
    )
    st3 = exchange(st3)
    mid, e2, st4, we2 = call(
        kern(middle_kernel), 11, [big_f, big_f, st8, square], [big_f, big_b, wide, tile8],
        z1, xp, ws1, st1, st3, row(lvgain_one), row(lvbias_one), row(scgain_one), row(scbias_one), enter2_f,
    )
    st4 = exchange(st4)
    g2, st5, bd2 = call(
        kern(conv_two_kernel), 13, [big_f, st8, blocks], [((3,) + slab, BF16), vbuf, wide_g, tile8],
        e2, st4, group2_f, row(engain_two), row(enbias_two),
    )
    st5 = exchange(st5)
    z2, st6, pool2, gate2, up2, wl2 = call(
        kern(leave_kernel), 9,
        [big_f, st8, pool_f, pool_f, ((SE_TWO, WIDTH), BF16), square],
        [big_f, big_b, wide, tile8],
        g2, st5, down2, row(sqdbias_two), up2_f, row(squbias_two), leave2_f, row(grgain_two), row(grbias_two),
    )
    st6 = exchange(st6)
    big_out, small_out, ds2, st7 = call(
        kern(final_kernel), 9, [(big_cot.shape, BF16), (small_cot.shape, BF16), big_f, st8],
        [big_f, tile8], z2, mid, st6, row(lvgain_two), row(lvbias_two), big_cot, small_cot,
    )
    st7 = exchange(st7)
    flat512 = ((4 * WIDTH, 128), F32)
    dy5, st8_, dleave2, ddown2, dup2, dlg2, dlb2 = call(
        kern(leave_two_back_kernel), 15,
        [big_f, st16, flat512, ((WIDTH, SE_TWO), F32), ((4 * SE_TWO, 128), F32), one_row, one_row],
        [big_b, big_f, big_f, big_b, big_f, pool_f, pool_f, tile16],
        z2, ds2, st6, st7, row(lvgain_two), g2, st5, row(grgain_two), row(grbias_two), pool2, gate2,
        down2, row(sqdbias_two), up2, row(squbias_two), wl2,
    )
    st8_ = exchange(st8_)
    dy4, st9, dgroup2, dgg2, dgb2, ddb2, dub2 = call(
        kern(conv_two_back_kernel), 22,
        [big_f, st8, ((9 * HALF, 128), F32), one_row, one_row, ((1, SE_TWO), F32), one_row],
        [((3,) + slab, BF16), ((3,) + slab, BF16), ((WIDTH, g.vwide), BF16), vbuf, big_f, wide_g, tile8],
        dy5, g2, st5, st8_, row(grgain_two), e2, st4, row(engain_two), row(enbias_two), bd2,
    )
    st9 = exchange(st9)
    d1, st10, denter2, deg2, deb2 = call(
        kern(enter_two_back_kernel), 16, [big_f, st16, flat512, one_row, one_row],
        [big_b, big_b, big_f, big_f, tile16],
        dy4, e2, st4, st9, row(engain_two), mid, ds2, we2, z1, st3, xp, ws1, st1,
        row(lvgain_one), row(lvbias_one), row(scgain_one), row(scbias_one),
    )
    st10 = exchange(st10)
    second = scatter_sums(nd, [denter2, dgroup2, ddown2, dup2, dleave2])
    dy2, st11, dsk, dleave1, dshort, ddown1, dup1, dlg1, dlb1, dsg1 = call(
        kern(leave_one_back_kernel), 18,
        [big_f, st16, big_b, flat512, ((4 * C_IN, 128), F32), ((WIDTH, SE_ONE), F32),
         ((4 * SE_ONE, 128), F32), one_row, one_row, one_row],
        [big_b, big_f, big_f, big_f, big_b, big_f, pool_f, pool_f, tile16],
        d1, z1, st3, xp, ws1, st1, st10, row(lvgain_one), row(scgain_one), g1, st2, row(grgain_one),
        row(grbias_one), pool1, gate1, down1, row(sqdbias_one), up1, row(squbias_one), wl1,
    )
    st11 = exchange(st11)
    dy1, st12, dgroup1, dgg1, dgb1, ddb1, dub1 = call(
        kern(conv_one_back_kernel), 33,
        [((4, g.rows, WIDTH), BF16), st8, ((9 * HALF, 128), F32), one_row, one_row, ((1, SE_ONE), F32), one_row],
        [((6,) + slab, BF16), ((2,) + slab, BF16), ((WIDTH, g.vwide), BF16), vbuf, big_f, big_f, wide_g, tile8],
        dy2, g1, st2, st11, row(grgain_one), xp, we1, st1, row(engain_one), row(enbias_one), bd1,
    )
    st12 = exchange(st12)
    dbig, dsmall, denter1, deg1, deb1 = call(
        kern(enter_one_back_kernel), 20,
        [(big_crops.shape, BF16), (small_crops.shape, BF16), ((4 * C_IN, 128), F32), one_row, one_row],
        [big_f, big_b, ((4, g.rows, C_IN), F32), ((2, 32, 128), F32)],
        dy1, xp, we1, st1, st12, row(engain_one), dsk, ws1,
    )
    first = scatter_sums(nd, [dgroup1, ddown1, dup1, dleave1, dshort])
    (denter,) = scatter_sums(nd, [denter1])
    vec = lambda v: v.reshape(-1)
    return (
        big_out, small_out, dbig, dsmall,
        denter, vec(deg1), vec(deb1), first[0], vec(dgg1), vec(dgb1), first[1], vec(ddb1), first[2],
        vec(dub1), first[3], vec(dlg1), vec(dlb1), first[4], vec(dsg1), vec(dlb1),
        second[0], vec(deg2), vec(deb2), second[1], vec(dgg2), vec(dgb2), second[2], vec(ddb2),
        second[3], vec(dub2), second[4], vec(dlg2), vec(dlb2),
    )


def solution(mesh):
    image = P(AXES, None, None, None)
    flat = P(AXES)
    whole = P()
    first = (flat, whole, whole, flat, whole, whole, flat, whole, flat, whole, flat, whole, whole)
    short = (flat, whole, whole)
    specs = (image,) * 4 + first + short + first
    return jax.shard_map(
        per_device, mesh=mesh, in_specs=specs, out_specs=specs, check_vma=False
    )
```
